128 devices in a mesh: row: 8 (over y, z_lo), col: 16 (over x, z_hi, core).
Axes of the slice: x: 4, y: 4, z: 4 (z_hi: 2, z_lo: 2; z = z_hi * 2 + z_lo), core: 2. Of those that a mesh axis runs over, the one named last changes fastest.
Arguments:
- tokens: bfloat16 [4096, 4608], P(('row', 'col')), may hold values from -6 to 6
- pre_gain: float32 [4608], replicated, may hold values from 0.25 to 1.75
- post_gain: float32 [4608], replicated, may hold values from 0.25 to 1.75
- gate_weight: bfloat16 [4608, 18432], P('row', 'col'), may hold values from -0.09375 to 0.09375
- up_weight: bfloat16 [4608, 18432], P('row', 'col'), may hold values from -0.09375 to 0.09375
- down_weight: bfloat16 [18432, 4608], P('col', 'row'), may hold values from -0.046875 to 0.046875
Outputs:
- mixed: bfloat16 [4096, 4608], P(('row', 'col'))
The draws below stay inside these ranges and needn't reach their ends.
All inputs are finite; a program needn't handle non-finite values.
Results may differ from the reference program's by a relative error of at most 0.015.
Values may be sent and summed in bfloat16 or wider, within the bound.
No kernel may reach another device: no remote copies, remote signals or barrier semaphores. Data moves between devices by JAX's collectives and lax.ppermute only.
A program may use at most 128 MiB of HBM per device.

```python
import jax
import jax.numpy as jnp
from jax import lax

D = 4608
FF = 18432
TOKENS = 4096


def block_scale(key, extent, split, low, largest):
    loudness, own = 1.0, jax.random.fold_in(key, 6)
    for axis_at, blocks in split:
        heights = jnp.exp(jax.random.uniform(jax.random.fold_in(own, axis_at), (blocks,), jnp.float32, low / len(split), largest / len(split)))
        loudness = loudness * jnp.repeat(heights, extent[axis_at] // blocks).reshape([-1 if axis == axis_at else 1 for axis in range(len(extent))])
    return loudness


def bell_draw(rng, dims, scale, bound, shards=(), dtype=jnp.bfloat16):
    entries = jax.random.normal(rng, dims, jnp.float32) * scale
    if len(shards) > 0:
        entries = block_scale(rng, dims, shards, -0.22, 0.18) * entries
    return jnp.clip(entries, min=-bound, max=bound).astype(dtype)


def setup_inputs(seed: int = 0) -> dict:
    arg_keys = jax.random.split(jax.random.key(seed), 7)
    tokens = bell_draw(arg_keys[0], (TOKENS, D), 1.0, 6.0, ((0, 128),))
    pre_gain = jnp.clip(1.0 + 0.15 * jax.random.normal(arg_keys[1], (D,), jnp.float32), 0.25, 1.75)
    post_gain = jnp.clip(1.0 + 0.15 * jax.random.normal(arg_keys[2], (D,), jnp.float32), 0.25, 1.75)
    gate_weight = bell_draw(arg_keys[3], (D, FF), D ** -0.5, 0.09375, ((0, 8), (1, 16)))
    up_weight = bell_draw(arg_keys[4], (D, FF), D ** -0.5, 0.09375, ((0, 8), (1, 16)))
    down_weight = bell_draw(arg_keys[5], (FF, D), FF ** -0.5, 0.046875, ((0, 16), (1, 8)))
    return {"tokens": tokens, "pre_gain": pre_gain, "post_gain": post_gain, "gate_weight": gate_weight, "up_weight": up_weight, "down_weight": down_weight}


def normalize(values, gain):
    widened = values.astype(jnp.float32)
    scale = lax.rsqrt(lax.optimization_barrier(jnp.mean(widened * widened, axis=-1, keepdims=True)) + 1e-06)
    return widened * scale * gain

def reference(tokens, pre_gain, post_gain, gate_weight, up_weight, down_weight):
    normed = normalize(tokens, pre_gain).astype(jnp.bfloat16)
    gate_values = jnp.dot(normed, gate_weight, preferred_element_type=jnp.float32)
    up_values = jnp.dot(normed, up_weight, preferred_element_type=jnp.float32)
    hidden = (jax.nn.gelu(gate_values, approximate=True) * up_values).astype(jnp.bfloat16)
    projected = jnp.dot(hidden, down_weight, preferred_element_type=jnp.float32).astype(jnp.bfloat16)
    mixed = tokens.astype(jnp.float32) + normalize(projected, post_gain)
    return mixed.astype(jnp.bfloat16)
```

```python
import jax
import jax.numpy as jnp
from jax import lax
from jax.sharding import PartitionSpec as P

AXES = ("row", "col")
EXTENT = {"y": 4, "zl": 2, "x": 4, "zh": 2, "core": 2}


def places():
    return [
        (y, zl, x, zh, core)
        for y in range(4)
        for zl in range(2)
        for x in range(4)
        for zh in range(2)
        for core in range(2)
    ]


def index(y, zl, x, zh, core):
    return (((y * 2 + zl) * 4 + x) * 2 + zh) * 2 + core


def send(values, move):
    return lax.ppermute(values, AXES, [(index(*at), index(*move(*at))) for at in places()])


def along_y(step):
    return lambda y, zl, x, zh, core: ((y + step) % 4, zl, x, zh, core)


def along_x(step):
    return lambda y, zl, x, zh, core: (y, zl, (x + step) % 4, zh, core)


def along_z(step):
    def move(y, zl, x, zh, core):
        z = (zh * 2 + zl + step) % 4
        return (y, z % 2, x, z // 2, core)

    return move


def other_core(y, zl, x, zh, core):
    return (y, zl, x, zh, 1 - core)


def turned(y, zl, x, zh, core):
    return (y, core, x, zh, zl)


def normalize(values, gain):
    widened = values.astype(jnp.float32)
    scale = lax.rsqrt(jnp.mean(widened * widened, axis=-1, keepdims=True) + 1e-06)
    return widened * scale * gain


def gather_weight(block):
    held = send(block, turned)
    before = send(held, along_y(1))
    after = send(held, along_y(-1))
    half = block.shape[0] // 2
    across = jnp.concatenate(
        [send(before[:half], along_y(1)), send(after[half:], along_y(-1))], axis=0
    )
    blocks = [held, after, across, before]
    return [jnp.concatenate([b, send(b, other_core)], axis=0) for b in blocks]


def on_device(tokens, pre_gain, post_gain, gate_weight, up_weight, down_weight):
    y = lax.axis_index("row") // 2
    zl = lax.axis_index("row") % 2
    core = lax.axis_index("col") % 2
    rows, width = tokens.shape
    block = width // 8

    normed = normalize(tokens, pre_gain).astype(jnp.bfloat16)
    normed = send(normed, turned).reshape(rows, 4, 2, block)
    normed = jnp.roll(jnp.roll(normed, -y, axis=1), -core, axis=2).reshape(rows, width)
    normed = jnp.concatenate(
        [normed] + [send(normed, along_x(-step)) for step in (1, 2, 3)], axis=0
    )
    normed = jnp.concatenate(
        [normed] + [send(normed, along_z(-step)) for step in (1, 2, 3)], axis=0
    )

    def project(pairs):
        return sum(
            jnp.dot(
                normed[:, j * 2 * block : (j + 1) * 2 * block],
                pair,
                preferred_element_type=jnp.float32,
            )
            for j, pair in enumerate(pairs)
        )

    gate_sum = project(gather_weight(gate_weight))
    up_sum = project(gather_weight(up_weight))
    hidden = (jax.nn.gelu(gate_sum, approximate=True) * up_sum).astype(jnp.bfloat16)

    parts = []
    for pair in gather_weight(down_weight.T):
        partial_value = lax.dot_general(
            hidden, pair, (((1,), (1,)), ((), ())), preferred_element_type=jnp.float32
        )
        for count, along in ((4, along_z), (4, along_x)):
            own = partial_value.shape[0] // count
            sent = partial_value.astype(jnp.bfloat16)
            partial_value = partial_value[:own]
            for step in range(1, count):
                arrived = send(sent[step * own : (step + 1) * own], along(step))
                partial_value = partial_value + arrived.astype(jnp.float32)
        parts.append(partial_value.astype(jnp.bfloat16))
    projected = send(jnp.concatenate(parts, axis=1), turned).reshape(rows, 4, 2, block)
    projected = jnp.roll(jnp.roll(projected, zl, axis=2), y, axis=1).reshape(rows, width)
    mixed = tokens.astype(jnp.float32) + normalize(projected, post_gain)
    return mixed.astype(jnp.bfloat16)


def solution(mesh):
    in_specs = (
        P(("row", "col"), None),
        P(),
        P(),
        P("row", "col"),
        P("row", "col"),
        P("col", "row"),
    )
    out_specs = P(("row", "col"), None)
    return jax.shard_map(
        on_device, mesh=mesh, in_specs=in_specs, out_specs=out_specs, check_vma=False
    )
```

```python
import jax
import jax.numpy as jnp
from jax import lax
from jax.sharding import PartitionSpec as P

AXES = ("row", "col")
EXTENT = {"y": 4, "zl": 2, "x": 4, "zh": 2, "core": 2}


def places():
    return [
        (y, zl, x, zh, core)
        for y in range(4)
        for zl in range(2)
        for x in range(4)
        for zh in range(2)
        for core in range(2)
    ]


def index(y, zl, x, zh, core):
    return (((y * 2 + zl) * 4 + x) * 2 + zh) * 2 + core


def send(values, move, chosen=lambda *at: True):
    pairs = [(index(*at), index(*move(*at))) for at in places() if chosen(*at)]
    return lax.ppermute(values, AXES, pairs)


def ordered(values, *earlier):
    return lax.optimization_barrier((values, *earlier))[0]


def along_y(step):
    return lambda y, zl, x, zh, core: ((y + step) % 4, zl, x, zh, core)


def along_x(step):
    return lambda y, zl, x, zh, core: (y, zl, (x + step) % 4, zh, core)


def along_z(low, high):
    return lambda y, zl, x, zh, core: (y, zl ^ low, x, zh ^ high, core)


def other_core(y, zl, x, zh, core):
    return (y, zl, x, zh, 1 - core)


def turned(y, zl, x, zh, core):
    return (y, core, x, zh, zl)


def normalize(values, gain):
    widened = values.astype(jnp.float32)
    scale = lax.rsqrt(jnp.mean(widened * widened, axis=-1, keepdims=True) + 1e-06)
    return widened * scale * gain


def straight(y, zl, x, zh, core):
    return zl == core


def crossed(y, zl, x, zh, core):
    return zl != core


def tied(*values):
    return lax.optimization_barrier(values)


def shared(y, zl, x, zh, core):
    return (y, 1 - core, x, zh, zl)


def scatter_x(sums):
    sent = sums.astype(jnp.bfloat16)
    total = sums[:, :, 0]
    for step in (1, 3, 2):
        total = total + send(sent[:, :, step], along_x(step)).astype(jnp.float32)
    return total


def scatter_high(sums):
    arrived = send(sums[:, 1].astype(jnp.bfloat16), along_z(0, 1))
    return sums[:, 0] + arrived.astype(jnp.float32)


def on_device(tokens, pre_gain, post_gain, gate_weight, up_weight, down_weight):
    y = lax.axis_index("row") // 2
    zl = lax.axis_index("row") % 2
    core = lax.axis_index("col") % 2
    rows, width = tokens.shape
    block = width // 8
    count = 16 * rows
    half = block // 2
    down_weight = down_weight.T

    def turn(values):
        return jnp.where(zl == core, values, send(values, turned, crossed))

    early = [send(gate_weight, along_y(step), straight) for step in (1, -1)]
    gate_turned = send(gate_weight, turned, crossed)
    normed = normalize(tokens, pre_gain).astype(jnp.bfloat16)
    normed = jnp.roll(normed.reshape(rows, 4, 2, block), -y, axis=1)
    kept = jnp.where(core == 0, normed[:, :, 0], normed[:, :, 1]).reshape(rows, 4 * block)
    given = jnp.where(core == 0, normed[:, :, 1], normed[:, :, 0]).reshape(rows, 4 * block)
    kept_1, kept_3 = (send(kept, along_x(-step)) for step in (1, 3))
    kept_2 = send(ordered(kept, kept_1), along_x(-2))
    early_1, early_3, gate_turned, kept, kept_1, kept_2, kept_3, given, up_weight = tied(
        *early, gate_turned, kept, kept_1, kept_2, kept_3, given, up_weight
    )

    late = [send(gate_turned, along_y(step), crossed) for step in (1, -1)]
    given_l, given_b = (send(given, along_z(1, high)) for high in (0, 1))
    given_h = send(ordered(given, given_b), along_z(0, 1))
    up_turned = send(up_weight, turned, crossed)
    kept = jnp.stack([kept, kept_1, kept_2, kept_3])
    late_1, late_3, up_turned, given, given_l, given_h, given_b, kept = tied(
        *late, up_turned, given, given_l, given_h, given_b, kept
    )
    given = jnp.stack([given, given_h, given_l, given_b])
    gate_held = jnp.where(zl == core, gate_weight, gate_turned)
    up_held = jnp.where(zl == core, up_weight, up_turned)
    gate_before = jnp.where(zl == core, early_1, late_1)
    gate_after = jnp.where(zl == core, early_3, late_3)

    up_before, up_after = (send(up_held, along_y(step)) for step in (1, -1))
    given_1, given_3 = (send(given, along_x(-step)) for step in (1, 3))
    kept_h = send(kept, along_z(0, 1))
    kept_later, given_later = tied(kept, given, given_1, given_3, kept_h)[:2]
    given_2 = send(given_later, along_x(-2))
    kept_l, kept_b = (send(kept_later, along_z(1, high)) for high in (0, 1))
    (
        up_before, up_after, gate_before, gate_after, down_weight,
        kept, kept_h, kept_l, kept_b, given, given_1, given_2, given_3,
    ) = tied(
        up_before, up_after, gate_before, gate_after, down_weight,
        kept, kept_h, kept_l, kept_b, given, given_1, given_2, given_3,
    )
    kept = jnp.stack([kept, kept_h, kept_l, kept_b]).reshape(count, 4 * block)
    given = jnp.stack([given, given_1, given_2, given_3], axis=1).reshape(count, 4 * block)

    gate_far = [send(gate_before[:half], along_y(1)), send(gate_after[half:], along_y(-1))]
    up_far = [send(up_before[:half], along_y(1)), send(up_after[half:], along_y(-1))]
    taken = send(given, other_core)
    *far, down_weight, taken = tied(*gate_far, *up_far, down_weight, taken)
    gathered = jnp.concatenate([kept, taken], axis=0)
    gate_across = jnp.concatenate(far[:2], axis=0)
    up_across = jnp.concatenate(far[2:], axis=0)

    down_before, down_after = (send(down_weight, along_y(step)) for step in (1, -1))
    down_across = jnp.concatenate(
        [send(down_before[:half], along_y(1)), send(down_after[half:], along_y(-1))], axis=0
    )

    def project(*blocks):
        sums = sum(
            jnp.dot(
                gathered[:, j * 2 * block : (j + 1) * 2 * block],
                jnp.concatenate(pair, axis=0),
                preferred_element_type=jnp.float32,
            )
            for j, pair in enumerate((blocks[:2], blocks[2:]))
        )
        arrived = send(sums[count:].astype(jnp.bfloat16), other_core)
        return sums[:count] + arrived.astype(jnp.float32)

    gate_sum = project(gate_held, gate_after, gate_across, gate_before)
    up_sum = project(up_held, up_after, up_across, up_before)
    hidden = (jax.nn.gelu(gate_sum, approximate=True) * up_sum).astype(jnp.bfloat16)

    crosswise = send(hidden, turned, crossed)
    second = send(hidden, shared)
    mine = jnp.where(zl == core, hidden, second)
    others = jnp.where(zl == core, second, crosswise).reshape(2, count // 2, -1)
    rows_in = jnp.concatenate([mine, others[1], others[0]], axis=0)

    def contribute(*pair):
        sums = lax.dot_general(
            rows_in,
            jnp.concatenate(pair, axis=0),
            (((1,), (1,)), ((), ())),
            preferred_element_type=jnp.float32,
        )
        arrived = send(sums[count:].astype(jnp.bfloat16), other_core)
        sums = sums[:count] + arrived.astype(jnp.float32)
        return sums.reshape(2, 2, 4, rows, 2 * block)

    near = scatter_x(scatter_high(contribute(down_weight, down_after))[:, None])[:, 0]
    far = scatter_high(scatter_x(contribute(down_across, down_before)))
    sums = jnp.concatenate([near, far], axis=2).astype(jnp.bfloat16)
    kept = jnp.where(zl == core, sums[0], sums[1]).reshape(rows, 4, block)
    given = jnp.where(zl == core, sums[1], sums[0])
    taken = send(given, along_z(1, 0)).reshape(rows, 4, block)
    projected = jnp.stack(
        [jnp.where(zl == 0, kept, taken), jnp.where(zl == 0, taken, kept)], axis=2
    )
    projected = jnp.roll(projected, y, axis=1).reshape(rows, width)
    mixed = tokens.astype(jnp.float32) + normalize(projected, post_gain)
    return mixed.astype(jnp.bfloat16)


def solution(mesh):
    in_specs = (
        P(("row", "col"), None),
        P(),
        P(),
        P("row", "col"),
        P("row", "col"),
        P("col", "row"),
    )
    out_specs = P(("row", "col"), None)
    return jax.shard_map(
        on_device, mesh=mesh, in_specs=in_specs, out_specs=out_specs, check_vma=False
    )
```

```python
import jax
import jax.numpy as jnp
from jax import lax
from jax.sharding import Mesh
from jax.sharding import PartitionSpec as P

AXES = ("y", "zl", "x", "zh", "core")
EXTENT = (4, 2, 4, 2, 2)


def places():
    return [
        (y, zl, x, zh, core)
        for y in range(4)
        for zl in range(2)
        for x in range(4)
        for zh in range(2)
        for core in range(2)
    ]


def index(y, zl, x, zh, core):
    return (((y * 2 + zl) * 4 + x) * 2 + zh) * 2 + core


def send(values, move, chosen=lambda *at: True):
    pairs = [(index(*at), index(*move(*at))) for at in places() if chosen(*at)]
    return lax.ppermute(values, AXES, pairs)


def along_y(step):
    return lambda y, zl, x, zh, core: ((y + step) % 4, zl, x, zh, core)


def along_x(step):
    return lambda y, zl, x, zh, core: (y, zl, (x + step) % 4, zh, core)


def along_z(low, high):
    return lambda y, zl, x, zh, core: (y, zl ^ low, x, zh ^ high, core)


def other_core(y, zl, x, zh, core):
    return (y, zl, x, zh, 1 - core)


def turned(y, zl, x, zh, core):
    return (y, core, x, zh, zl)


def normalize(values, gain):
    widened = values.astype(jnp.float32)
    scale = lax.rsqrt(jnp.mean(widened * widened, axis=-1, keepdims=True) + 1e-06)
    return widened * scale * gain


def crossed(y, zl, x, zh, core):
    return zl != core


def tied(*values):
    return lax.optimization_barrier(values)


def shared(y, zl, x, zh, core):
    return (y, 1 - core, x, zh, zl)


def scatter_x(sums):
    sent = sums.astype(jnp.bfloat16)
    total = sums[:, :, 0]
    for step in (1, 3, 2):
        total = total + send(sent[:, :, step], along_x(step)).astype(jnp.float32)
    return total


def scatter_high(sums):
    arrived = send(sums[:, 1].astype(jnp.bfloat16), along_z(0, 1))
    return sums[:, 0] + arrived.astype(jnp.float32)


def on_device(tokens, pre_gain, post_gain, gate_weight, up_weight, down_weight):
    y, zl, core = (lax.axis_index(axis) for axis in ("y", "zl", "core"))
    rows, width = tokens.shape
    block = width // 8
    count = 16 * rows
    half = block // 2
    down_weight = down_weight.T

    down_before, down_after = (send(down_weight, along_y(step)) for step in (1, -1))
    gate_turned = send(gate_weight, turned, crossed)
    normed = normalize(tokens, pre_gain).astype(jnp.bfloat16)
    normed = jnp.roll(normed.reshape(rows, 4, 2, block), -y, axis=1)
    normed = jnp.concatenate([normed[:, :2], normed[:, 3:], normed[:, 2:3]], axis=1)
    kept = jnp.where(core == 0, normed[:, :, 0], normed[:, :, 1]).reshape(rows, 4 * block)
    given = jnp.where(core == 0, normed[:, :, 1], normed[:, :, 0]).reshape(rows, 4 * block)
    given_b = send(given, along_z(1, 1))
    kept_1 = send(kept, along_x(-1))
    given_h, given_l = send(given, along_z(0, 1)), send(given, along_z(1, 0))
    (
        down_before, down_after, gate_turned, up_weight,
        kept, kept_1, given, given_l, given_h, given_b,
    ) = tied(
        down_before, down_after, gate_turned, up_weight,
        kept, kept_1, given, given_l, given_h, given_b,
    )

    gate_held = jnp.where(zl == core, gate_weight, gate_turned)
    gate_before, gate_after = (send(gate_held, along_y(step)) for step in (1, -1))
    up_turned = send(up_weight, turned, crossed)
    kept_2, kept_3 = (send(kept, along_x(-step)) for step in (2, 3))
    given = jnp.stack([given, given_h, given_l, given_b])
    given_1, given_3 = (send(given, along_x(-step)) for step in (1, 3))
    (
        gate_before, gate_after, up_turned,
        kept, kept_1, kept_2, kept_3, given, given_1, given_3,
    ) = tied(
        gate_before, gate_after, up_turned,
        kept, kept_1, kept_2, kept_3, given, given_1, given_3,
    )

    up_held = jnp.where(zl == core, up_weight, up_turned)
    up_before, up_after = (send(up_held, along_y(step)) for step in (1, -1))
    kept = jnp.stack([kept, kept_1, kept_2, kept_3])
    kept_l, kept_h, kept_b = (
        send(kept, along_z(low, high)) for low, high in ((1, 0), (0, 1), (1, 1))
    )
    given_2 = send(given, along_x(-2))
    (
        up_before, up_after, gate_before, gate_after,
        kept, kept_l, kept_h, kept_b, given, given_1, given_2, given_3,
    ) = tied(
        up_before, up_after, gate_before, gate_after,
        kept, kept_l, kept_h, kept_b, given, given_1, given_2, given_3,
    )

    gate_far = [send(gate_before[:half], along_y(1)), send(gate_after[half:], along_y(-1))]
    up_far = [send(up_before[:half], along_y(1)), send(up_after[half:], along_y(-1))]
    kept = jnp.stack([kept, kept_h, kept_l, kept_b]).reshape(count, 4 * block)
    given = jnp.stack([given, given_1, given_2, given_3], axis=1)
    taken = send(given.reshape(count, 4 * block), other_core)
    gathered = jnp.concatenate([kept, taken], axis=0)

    def product(low, *blocks):
        return jnp.dot(
            gathered[:, low * block : (low + len(blocks)) * block],
            jnp.concatenate(blocks, axis=0),
            preferred_element_type=jnp.float32,
        )

    gate_sum = product(0, gate_held, gate_after) + product(2, gate_before)
    up_sum = product(0, up_held, up_after) + product(2, up_before)
    last = gathered[:, 3 * block :]
    *far, gate_sum, up_sum, last, down_before, down_after = tied(
        *gate_far, *up_far, gate_sum, up_sum, last, down_before, down_after
    )

    down_far = [send(down_before[:half], along_y(1)), send(down_after[half:], along_y(-1))]

    def complete(sums, *halves):
        sums = sums + jnp.dot(
            last, jnp.concatenate(halves, axis=0), preferred_element_type=jnp.float32
        )
        arrived = send(sums[count:].astype(jnp.bfloat16), other_core)
        return sums[:count] + arrived.astype(jnp.float32)

    gate_sum = complete(gate_sum, *far[:2])
    up_sum = complete(up_sum, *far[2:])
    hidden = (jax.nn.gelu(gate_sum, approximate=True) * up_sum).astype(jnp.bfloat16)

    crosswise = send(hidden, turned, crossed)
    second = send(hidden, shared)
    mine = jnp.where(zl == core, hidden, second)
    others = jnp.where(zl == core, second, crosswise).reshape(2, count // 2, -1)
    rows_in = jnp.concatenate([mine, others[1], others[0]], axis=0)

    def contribute(rows_in, *pair):
        sums = lax.dot_general(
            rows_in,
            jnp.concatenate(pair, axis=0),
            (((1,), (1,)), ((), ())),
            preferred_element_type=jnp.float32,
        )
        arrived = send(sums[count:].astype(jnp.bfloat16), other_core)
        sums = sums[:count] + arrived.astype(jnp.float32)
        return sums.reshape(2, 2, 4, rows, 2 * block)

    near = contribute(rows_in, down_weight, down_after)
    far = contribute(rows_in, *down_far, down_before)
    near, far = scatter_high(near), scatter_x(far)
    near, far = scatter_x(near[:, None])[:, 0], scatter_high(far)
    sums = jnp.concatenate([near, far], axis=2).astype(jnp.bfloat16)
    kept = jnp.where(zl == core, sums[0], sums[1]).reshape(rows, 4, block)
    given = jnp.where(zl == core, sums[1], sums[0])
    taken = send(given, along_z(1, 0)).reshape(rows, 4, block)
    projected = jnp.stack(
        [jnp.where(zl == 0, kept, taken), jnp.where(zl == 0, taken, kept)], axis=2
    )
    projected = jnp.roll(projected, y, axis=1).reshape(rows, width)
    mixed = tokens.astype(jnp.float32) + normalize(projected, post_gain)
    return mixed.astype(jnp.bfloat16)


def solution(mesh):
    mesh = Mesh(mesh.devices.reshape(EXTENT), AXES)
    row, col = ("y", "zl"), ("x", "zh", "core")
    in_specs = (P(row + col, None), P(), P(), P(row, col), P(row, col), P(col, row))
    out_specs = P(row + col, None)
    return jax.shard_map(
        on_device, mesh=mesh, in_specs=in_specs, out_specs=out_specs, check_vma=False
    )
```

```python
import jax
import jax.numpy as jnp
from jax import lax
from jax.sharding import Mesh
from jax.sharding import PartitionSpec as P

AXES = ("y", "zl", "x", "zh", "core")
EXTENT = (4, 2, 4, 2, 2)


def places():
    return [
        (y, zl, x, zh, core)
        for y in range(4)
        for zl in range(2)
        for x in range(4)
        for zh in range(2)
        for core in range(2)
    ]


def index(y, zl, x, zh, core):
    return (((y * 2 + zl) * 4 + x) * 2 + zh) * 2 + core


def send(values, move, chosen=lambda *at: True):
    pairs = [(index(*at), index(*move(*at))) for at in places() if chosen(*at)]
    return lax.ppermute(values, AXES, pairs)


def along_y(step):
    return lambda y, zl, x, zh, core: ((y + step) % 4, zl, x, zh, core)


def along_x(step):
    return lambda y, zl, x, zh, core: (y, zl, (x + step) % 4, zh, core)


def along_z(low, high):
    return lambda y, zl, x, zh, core: (y, zl ^ low, x, zh ^ high, core)


def other_core(y, zl, x, zh, core):
    return (y, zl, x, zh, 1 - core)


def turned(y, zl, x, zh, core):
    return (y, core, x, zh, zl)


def normalize(values, gain):
    widened = values.astype(jnp.float32)
    scale = lax.rsqrt(jnp.mean(widened * widened, axis=-1, keepdims=True) + 1e-06)
    return widened * scale * gain


def crossed(y, zl, x, zh, core):
    return zl != core


def tied(*values):
    return lax.optimization_barrier(values)


def shared(y, zl, x, zh, core):
    return (y, 1 - core, x, zh, zl)


def scatter_x(sums):
    sent = sums.astype(jnp.bfloat16)
    total = sums[:, :, 0]
    for step in (1, 3, 2):
        total = total + send(sent[:, :, step], along_x(step)).astype(jnp.float32)
    return total


def scatter_high(sums):
    arrived = send(sums[:, 1].astype(jnp.bfloat16), along_z(0, 1))
    return sums[:, 0] + arrived.astype(jnp.float32)


def on_device(tokens, pre_gain, post_gain, gate_weight, up_weight, down_weight):
    y, zl, core = (lax.axis_index(axis) for axis in ("y", "zl", "core"))
    rows, width = tokens.shape
    block = width // 8
    count = 16 * rows
    half = block // 2
    down_weight = down_weight.T

    down_before, down_after = (send(down_weight, along_y(step)) for step in (1, -1))
    gate_turned = send(gate_weight, turned, crossed)
    normed = normalize(tokens, pre_gain).astype(jnp.bfloat16)
    normed = jnp.roll(normed.reshape(rows, 4, 2, block), -y, axis=1)
    normed = jnp.concatenate([normed[:, :2], normed[:, 3:], normed[:, 2:3]], axis=1)
    kept = jnp.where(core == 0, normed[:, :, 0], normed[:, :, 1]).reshape(rows, 4 * block)
    given = jnp.where(core == 0, normed[:, :, 1], normed[:, :, 0]).reshape(rows, 4 * block)
    given_b = send(given, along_z(1, 1))
    kept_1 = send(kept, along_x(-1))
    given_h, given_l = send(given, along_z(0, 1)), send(given, along_z(1, 0))
    (
        down_before, down_after, gate_turned, up_weight,
        kept, kept_1, given, given_l, given_h, given_b,
    ) = tied(
        down_before, down_after, gate_turned, up_weight,
        kept, kept_1, given, given_l, given_h, given_b,
    )

    gate_held = jnp.where(zl == core, gate_weight, gate_turned)
    gate_before, gate_after = (send(gate_held, along_y(step)) for step in (1, -1))
    up_turned = send(up_weight, turned, crossed)
    kept_2, kept_3 = (send(kept, along_x(-step)) for step in (2, 3))
    given = jnp.stack([given, given_h, given_l, given_b])
    given_1, given_3 = (send(given, along_x(-step)) for step in (1, 3))
    (
        gate_before, gate_after, up_turned,
        kept, kept_1, kept_2, kept_3, given, given_1, given_3,
    ) = tied(
        gate_before, gate_after, up_turned,
        kept, kept_1, kept_2, kept_3, given, given_1, given_3,
    )

    up_held = jnp.where(zl == core, up_weight, up_turned)
    up_before, up_after = (send(up_held, along_y(step)) for step in (1, -1))
    kept = jnp.stack([kept, kept_1, kept_2, kept_3])
    kept_l, kept_h, kept_b = (
        send(kept, along_z(low, high)) for low, high in ((1, 0), (0, 1), (1, 1))
    )
    given_2 = send(given, along_x(-2))
    (
        up_before, up_after, gate_before, gate_after,
        kept, kept_l, kept_h, kept_b, given, given_1, given_2, given_3,
    ) = tied(
        up_before, up_after, gate_before, gate_after,
        kept, kept_l, kept_h, kept_b, given, given_1, given_2, given_3,
    )

    gate_far = [send(gate_before[:half], along_y(1)), send(gate_after[half:], along_y(-1))]
    up_far = [send(up_before[:half], along_y(1)), send(up_after[half:], along_y(-1))]
    kept = jnp.stack([kept, kept_h, kept_l, kept_b]).reshape(count, 4 * block)
    given = jnp.stack([given, given_1, given_2, given_3], axis=1)
    taken = send(given.reshape(count, 4 * block), other_core)
    gathered = jnp.concatenate([kept, taken], axis=0)

    def product(low, *blocks):
        return jnp.dot(
            gathered[:, low * block : (low + len(blocks)) * block],
            jnp.concatenate(blocks, axis=0),
            preferred_element_type=jnp.float32,
        )

    gate_sum = product(0, gate_held, gate_after) + product(2, gate_before)
    up_sum = product(0, up_held, up_after) + product(2, up_before)
    last = gathered[:, 3 * block :]
    gate_last = last
    *up_far, up_sum, last, down_before, down_after = tied(
        *up_far, up_sum, last, down_before, down_after
    )

    down_far = [send(down_before[:half], along_y(1)), send(down_after[half:], along_y(-1))]

    def complete(sums, last, *halves):
        sums = sums + jnp.dot(
            last, jnp.concatenate(halves, axis=0), preferred_element_type=jnp.float32
        )
        arrived = send(sums[count:].astype(jnp.bfloat16), other_core)
        return sums[:count] + arrived.astype(jnp.float32)

    gate_sum = complete(gate_sum, gate_last, *gate_far)
    up_sum = complete(up_sum, last, *up_far)
    hidden = (jax.nn.gelu(gate_sum, approximate=True) * up_sum).astype(jnp.bfloat16)

    crosswise = send(hidden, turned, crossed)
    second = send(hidden, shared)
    mine = jnp.where(zl == core, hidden, second)
    others = jnp.where(zl == core, second, crosswise)
    others = jnp.roll(others, count // 2, axis=0)
    near = jnp.concatenate([down_weight, down_after], axis=0)
    far = jnp.concatenate([*down_far, down_before], axis=0)
    near, far = tied(near, hidden)[0], tied(far)[0]

    def give(rows_out):
        sums = lax.dot_general(
            others, rows_out, (((1,), (1,)), ((), ())), preferred_element_type=jnp.float32
        )
        return send(sums.astype(jnp.bfloat16), other_core)

    def keep(mine, rows_out, arrived):
        sums = lax.dot_general(
            mine, rows_out, (((1,), (1,)), ((), ())), preferred_element_type=jnp.float32
        )
        return (sums + arrived.astype(jnp.float32)).reshape(2, 2, 4, rows, 2 * block)

    near_sums = keep(mine, near, give(near))
    far_arrived = give(far)
    mine, near_sums = tied(mine, near_sums)
    near, far = scatter_high(near_sums), scatter_x(keep(mine, far, far_arrived))
    near, far = scatter_x(near[:, None])[:, 0], scatter_high(far)
    sums = jnp.concatenate([near, far], axis=2).astype(jnp.bfloat16)
    kept = jnp.where(zl == core, sums[0], sums[1]).reshape(rows, 4, block)
    given = jnp.where(zl == core, sums[1], sums[0])
    taken = send(given, along_z(1, 0)).reshape(rows, 4, block)
    projected = jnp.stack(
        [jnp.where(zl == 0, kept, taken), jnp.where(zl == 0, taken, kept)], axis=2
    )
    projected = jnp.roll(projected, y, axis=1).reshape(rows, width)
    mixed = tokens.astype(jnp.float32) + normalize(projected, post_gain)
    return mixed.astype(jnp.bfloat16)


def solution(mesh):
    mesh = Mesh(mesh.devices.reshape(EXTENT), AXES)
    row, col = ("y", "zl"), ("x", "zh", "core")
    in_specs = (P(row + col, None), P(), P(), P(row, col), P(row, col), P(col, row))
    out_specs = P(row + col, None)
    return jax.shard_map(
        on_device, mesh=mesh, in_specs=in_specs, out_specs=out_specs, check_vma=False
    )
```

```python
import jax
import jax.numpy as jnp
from jax import lax
from jax.sharding import Mesh
from jax.sharding import PartitionSpec as P

AXES = ("y", "zl", "x", "zh", "core")
EXTENT = (4, 2, 4, 2, 2)


def places():
    return [
        (y, zl, x, zh, core)
        for y in range(4)
        for zl in range(2)
        for x in range(4)
        for zh in range(2)
        for core in range(2)
    ]


def index(y, zl, x, zh, core):
    return (((y * 2 + zl) * 4 + x) * 2 + zh) * 2 + core


def send(values, move, chosen=lambda *at: True):
    pairs = [(index(*at), index(*move(*at))) for at in places() if chosen(*at)]
    return lax.ppermute(values, AXES, pairs)


def along_y(step):
    return lambda y, zl, x, zh, core: ((y + step) % 4, zl, x, zh, core)


def around_y(step):
    return lambda y, zl, x, zh, core: ((y + (step, -step)[core]) % 4, zl, x, zh, core)


def along_x(step):
    return lambda y, zl, x, zh, core: (y, zl, (x + step) % 4, zh, core)


def along_z(low, high):
    return lambda y, zl, x, zh, core: (y, zl ^ low, x, zh ^ high, core)


def other_core(y, zl, x, zh, core):
    return (y, zl, x, zh, 1 - core)


def turned(y, zl, x, zh, core):
    return (y, core, x, zh, zl)


def normalize(values, gain):
    widened = values.astype(jnp.float32)
    scale = lax.rsqrt(jnp.mean(widened * widened, axis=-1, keepdims=True) + 1e-06)
    return widened * scale * gain


def crossed(y, zl, x, zh, core):
    return zl != core


def tied(*values):
    return lax.optimization_barrier(values)


def shared(y, zl, x, zh, core):
    return (y, 1 - core, x, zh, zl)


def scatter_x(sums):
    sent = sums.astype(jnp.bfloat16)
    total = sums[:, :, 0]
    for step in (1, 3, 2):
        total = total + send(sent[:, :, step], along_x(step)).astype(jnp.float32)
    return total


def scatter_high(sums):
    arrived = send(sums[:, 1].astype(jnp.bfloat16), along_z(0, 1))
    return sums[:, 0] + arrived.astype(jnp.float32)


def on_device(tokens, pre_gain, post_gain, gate_weight, up_weight, down_weight):
    y, zl, core = (lax.axis_index(axis) for axis in ("y", "zl", "core"))
    rows, width = tokens.shape
    block = width // 8
    count = 16 * rows
    half = block // 2
    down_weight = down_weight.T

    down_before, down_after = (send(down_weight, along_y(step)) for step in (1, -1))
    gate_turned = send(gate_weight, turned, crossed)
    normed = normalize(tokens, pre_gain).astype(jnp.bfloat16)
    normed = jnp.roll(normed.reshape(rows, 4, 2, block), -y, axis=1)
    halves = [
        jnp.concatenate([normed[:, j, half_at] for j in order], axis=1)
        for half_at, order in enumerate(((0, 1, 3, 2), (0, 3, 1, 2)))
    ]
    kept = jnp.where(core == 0, *halves)
    given = jnp.where(core == 0, *halves[::-1])
    given_b = send(given, along_z(1, 1))
    kept_1 = send(kept, along_x(-1))
    given_h, given_l = send(given, along_z(0, 1)), send(given, along_z(1, 0))
    gate_held = jnp.where(zl == core, gate_weight, gate_turned)
    (
        down_before, down_after, gate_held, up_weight,
        kept, kept_1, given, given_l, given_h, given_b,
    ) = tied(
        down_before, down_after, gate_held, up_weight,
        kept, kept_1, given, given_l, given_h, given_b,
    )

    gate_before, gate_after = (send(gate_held, around_y(step)) for step in (1, -1))
    up_turned = send(up_weight, turned, crossed)
    kept_2, kept_3 = (send(kept, along_x(-step)) for step in (2, 3))
    given = jnp.stack([given, given_h, given_l, given_b])
    given_1, given_3 = (send(given, along_x(-step)) for step in (1, 3))
    (
        gate_before, gate_after, up_turned,
        kept, kept_1, kept_2, kept_3, given, given_1, given_3,
    ) = tied(
        gate_before, gate_after, up_turned,
        kept, kept_1, kept_2, kept_3, given, given_1, given_3,
    )

    up_held = jnp.where(zl == core, up_weight, up_turned)
    up_before, up_after = (send(up_held, around_y(step)) for step in (1, -1))
    kept = jnp.stack([kept, kept_1, kept_2, kept_3])
    kept_l, kept_h, kept_b = (
        send(kept, along_z(low, high)) for low, high in ((1, 0), (0, 1), (1, 1))
    )
    given_2 = send(given, along_x(-2))
    (
        up_before, up_after, gate_before, gate_after,
        kept, kept_l, kept_h, kept_b, given, given_1, given_2, given_3,
    ) = tied(
        up_before, up_after, gate_before, gate_after,
        kept, kept_l, kept_h, kept_b, given, given_1, given_2, given_3,
    )

    gate_far = [send(gate_before[:half], around_y(1)), send(gate_after[half:], around_y(-1))]
    up_far = [send(up_before[:half], around_y(1)), send(up_after[half:], around_y(-1))]
    kept = jnp.stack([kept, kept_h, kept_l, kept_b]).reshape(count, 4 * block)
    given = jnp.stack([given, given_1, given_2, given_3], axis=1)
    taken = send(given.reshape(count, 4 * block), other_core)
    gathered = jnp.concatenate([kept, taken], axis=0)

    def product(low, *blocks):
        return jnp.dot(
            gathered[:, low * block : (low + len(blocks)) * block],
            jnp.concatenate(blocks, axis=0),
            preferred_element_type=jnp.float32,
        )

    gate_sum = product(0, gate_held, gate_after) + product(2, gate_before)
    up_sum = product(0, up_held, up_after) + product(2, up_before)
    last = gathered[:, 3 * block :]
    gate_last = last
    *up_far, up_sum, last, down_before, down_after = tied(
        *up_far, up_sum, last, down_before, down_after
    )

    down_far = [send(down_before[:half], along_y(1)), send(down_after[half:], along_y(-1))]

    def complete(sums, last, *halves):
        sums = sums + jnp.dot(
            last, jnp.concatenate(halves, axis=0), preferred_element_type=jnp.float32
        )
        arrived = send(sums[count:].astype(jnp.bfloat16), other_core)
        return sums[:count] + arrived.astype(jnp.float32)

    gate_sum = complete(gate_sum, gate_last, *gate_far)
    up_sum = complete(up_sum, last, *up_far)
    hidden = (jax.nn.gelu(gate_sum, approximate=True) * up_sum).astype(jnp.bfloat16)

    crosswise = send(hidden, turned, crossed)
    second = send(hidden, shared)
    mine = jnp.where(zl == core, hidden, second)
    others = jnp.where(zl == core, second, crosswise)
    others = jnp.roll(others, count // 2, axis=0)
    near = jnp.concatenate([down_weight, down_after], axis=0)
    far = jnp.concatenate([*down_far, down_before], axis=0)
    near, far = tied(near, hidden)[0], tied(far)[0]

    def give(rows_out):
        sums = lax.dot_general(
            others, rows_out, (((1,), (1,)), ((), ())), preferred_element_type=jnp.float32
        )
        return send(sums.astype(jnp.bfloat16), other_core)

    def keep(mine, rows_out, arrived):
        sums = lax.dot_general(
            mine, rows_out, (((1,), (1,)), ((), ())), preferred_element_type=jnp.float32
        )
        return (sums + arrived.astype(jnp.float32)).reshape(2, 2, 4, rows, 2 * block)

    near_sums = keep(mine, near, give(near))
    far_arrived = give(far)
    mine, near_sums = tied(mine, near_sums)
    near, far = scatter_high(near_sums), scatter_x(keep(mine, far, far_arrived))
    near, far = scatter_x(near[:, None])[:, 0], scatter_high(far)
    sums = jnp.concatenate([near, far], axis=2).astype(jnp.bfloat16)
    kept = jnp.where(zl == core, sums[0], sums[1]).reshape(rows, 4, block)
    given = jnp.where(zl == core, sums[1], sums[0])
    taken = send(given, along_z(1, 0)).reshape(rows, 4, block)
    projected = jnp.stack(
        [jnp.where(zl == 0, kept, taken), jnp.where(zl == 0, taken, kept)], axis=2
    )
    projected = jnp.roll(projected, y, axis=1).reshape(rows, width)
    mixed = tokens.astype(jnp.float32) + normalize(projected, post_gain)
    return mixed.astype(jnp.bfloat16)


def solution(mesh):
    mesh = Mesh(mesh.devices.reshape(EXTENT), AXES)
    row, col = ("y", "zl"), ("x", "zh", "core")
    in_specs = (P(row + col, None), P(), P(), P(row, col), P(row, col), P(col, row))
    out_specs = P(row + col, None)
    return jax.shard_map(
        on_device, mesh=mesh, in_specs=in_specs, out_specs=out_specs, check_vma=False
    )
```

```python
import jax
import jax.numpy as jnp
from jax import lax
from jax.sharding import Mesh
from jax.sharding import PartitionSpec as P

AXES = ("y", "zl", "x", "zh", "core")
EXTENT = (4, 2, 4, 2, 2)


def places():
    return [
        (y, zl, x, zh, core)
        for y in range(4)
        for zl in range(2)
        for x in range(4)
        for zh in range(2)
        for core in range(2)
    ]


def index(y, zl, x, zh, core):
    return (((y * 2 + zl) * 4 + x) * 2 + zh) * 2 + core


def send(values, move, chosen=lambda *at: True):
    pairs = [(index(*at), index(*move(*at))) for at in places() if chosen(*at)]
    return lax.ppermute(values, AXES, pairs)


def along_y(step):
    return lambda y, zl, x, zh, core: ((y + step) % 4, zl, x, zh, core)


def around_y(step):
    return lambda y, zl, x, zh, core: ((y + (step, -step)[core]) % 4, zl, x, zh, core)


def along_x(step):
    return lambda y, zl, x, zh, core: (y, zl, (x + step) % 4, zh, core)


def along_z(low, high):
    return lambda y, zl, x, zh, core: (y, zl ^ low, x, zh ^ high, core)


def other_core(y, zl, x, zh, core):
    return (y, zl, x, zh, 1 - core)


def turned(y, zl, x, zh, core):
    return (y, core, x, zh, zl)


def normalize(values, gain):
    widened = values.astype(jnp.float32)
    scale = lax.rsqrt(jnp.mean(widened * widened, axis=-1, keepdims=True) + 1e-06)
    return widened * scale * gain


def crossed(y, zl, x, zh, core):
    return zl != core


def tied(*values):
    return lax.optimization_barrier(values)


def shared(y, zl, x, zh, core):
    return (y, 1 - core, x, zh, zl)


def scatter_x(sums):
    sent = sums.astype(jnp.bfloat16)
    total = sums[:, :, 0]
    for step in (1, 3, 2):
        total = total + send(sent[:, :, step], along_x(step)).astype(jnp.float32)
    return total


def scatter_high(sums):
    arrived = send(sums[:, 1].astype(jnp.bfloat16), along_z(0, 1))
    return sums[:, 0] + arrived.astype(jnp.float32)


def on_device(tokens, pre_gain, post_gain, gate_weight, up_weight, down_weight):
    y, zl, core = (lax.axis_index(axis) for axis in ("y", "zl", "core"))
    rows, width = tokens.shape
    block = width // 8
    count = 16 * rows
    half = block // 2
    down_weight = down_weight.T

    down_before, down_after = (send(down_weight, along_y(step)) for step in (1, -1))
    gate_turned = send(gate_weight, turned, crossed)
    normed = normalize(tokens, pre_gain).astype(jnp.bfloat16)
    normed = jnp.roll(normed.reshape(rows, 4, 2, block), -y, axis=1)
    halves = [
        jnp.concatenate([normed[:, j, half_at] for j in order], axis=1)
        for half_at, order in enumerate(((0, 1, 3, 2), (0, 3, 1, 2)))
    ]
    kept = jnp.where(core == 0, *halves)
    given = jnp.where(core == 0, *halves[::-1])
    given_b = send(given, along_z(1, 1))
    kept_1 = send(kept, along_x(-1))
    given_h, given_l = send(given, along_z(0, 1)), send(given, along_z(1, 0))
    gate_held = jnp.where(zl == core, gate_weight, gate_turned)
    (
        down_before, down_after, gate_held, up_weight,
        kept, kept_1, given, given_l, given_h, given_b,
    ) = tied(
        down_before, down_after, gate_held, up_weight,
        kept, kept_1, given, given_l, given_h, given_b,
    )

    gate_before, gate_after = (send(gate_held, around_y(step)) for step in (1, -1))
    up_turned = send(up_weight, turned, crossed)
    kept_2, kept_3 = (send(kept, along_x(-step)) for step in (2, 3))
    given = jnp.stack([given, given_h, given_l, given_b])
    given_1, given_3 = (send(given, along_x(-step)) for step in (1, 3))
    (
        gate_before, gate_after, up_turned,
        kept, kept_1, kept_2, kept_3, given, given_1, given_3,
    ) = tied(
        gate_before, gate_after, up_turned,
        kept, kept_1, kept_2, kept_3, given, given_1, given_3,
    )

    up_held = jnp.where(zl == core, up_weight, up_turned)
    up_before, up_after = (send(up_held, around_y(step)) for step in (1, -1))
    kept = jnp.stack([kept, kept_1, kept_2, kept_3])
    kept_l, kept_h, kept_b = (
        send(kept, along_z(low, high)) for low, high in ((1, 0), (0, 1), (1, 1))
    )
    given_2 = send(given, along_x(-2))
    (
        up_before, up_after, gate_before, gate_after,
        kept, kept_l, kept_h, kept_b, given, given_1, given_2, given_3,
    ) = tied(
        up_before, up_after, gate_before, gate_after,
        kept, kept_l, kept_h, kept_b, given, given_1, given_2, given_3,
    )

    gate_far = [send(gate_before[:half], around_y(1)), send(gate_after[half:], around_y(-1))]
    up_far = [send(up_before[:half], around_y(1)), send(up_after[half:], around_y(-1))]
    kept = jnp.stack([kept, kept_h, kept_l, kept_b]).reshape(count, 4 * block)
    given = jnp.stack([given, given_1, given_2, given_3], axis=1)
    taken = send(given.reshape(count, 4 * block), other_core)
    gathered = jnp.concatenate([kept, taken], axis=0)

    def product(low, *blocks):
        return jnp.dot(
            gathered[:, low * block : (low + len(blocks)) * block],
            jnp.concatenate(blocks, axis=0),
            preferred_element_type=jnp.float32,
        )

    gate_sum = product(0, gate_held, gate_after) + product(2, gate_before)
    up_sum = product(0, up_held, up_after) + product(2, up_before)
    last = gathered[:, 3 * block :]
    gate_last = last
    *up_far, up_sum, last, down_before, down_after = tied(
        *up_far, up_sum, last, down_before, down_after
    )

    down_far = [send(down_before[:half], along_y(1)), send(down_after[half:], along_y(-1))]

    def complete(sums, last, *halves):
        across = jnp.concatenate(halves, axis=0)
        sent, own = (
            sums[part] + jnp.dot(last[part], across, preferred_element_type=jnp.float32)
            for part in (slice(count, None), slice(0, count))
        )
        return own + send(sent.astype(jnp.bfloat16), other_core).astype(jnp.float32)

    gate_sum = complete(gate_sum, gate_last, *gate_far)
    up_sum = complete(up_sum, last, *up_far)
    hidden = (jax.nn.gelu(gate_sum, approximate=True) * up_sum).astype(jnp.bfloat16)

    crosswise = send(hidden, turned, crossed)
    second = send(hidden, shared)
    mine = jnp.where(zl == core, hidden, second)
    others = jnp.where(zl == core, second, crosswise)
    others = jnp.roll(others, count // 2, axis=0)
    near = jnp.concatenate([down_weight, down_after], axis=0)
    far = jnp.concatenate([*down_far, down_before], axis=0)
    near, far = tied(near, hidden)[0], tied(far)[0]

    def give(rows_out):
        sums = lax.dot_general(
            others, rows_out, (((1,), (1,)), ((), ())), preferred_element_type=jnp.float32
        )
        return send(sums.astype(jnp.bfloat16), other_core)

    def keep(mine, rows_out, arrived):
        sums = lax.dot_general(
            mine, rows_out, (((1,), (1,)), ((), ())), preferred_element_type=jnp.float32
        )
        return (sums + arrived.astype(jnp.float32)).reshape(2, 2, 4, rows, 2 * block)

    near_sums = keep(mine, near, give(near))
    far_arrived = give(far)
    mine, near_sums = tied(mine, near_sums)
    near, far = scatter_high(near_sums), scatter_x(keep(mine, far, far_arrived))
    near, far = scatter_x(near[:, None])[:, 0], scatter_high(far)
    sums = jnp.concatenate([near, far], axis=2).astype(jnp.bfloat16)
    kept = jnp.where(zl == core, sums[0], sums[1]).reshape(rows, 4, block)
    given = jnp.where(zl == core, sums[1], sums[0])
    taken = send(given, along_z(1, 0)).reshape(rows, 4, block)
    projected = jnp.stack(
        [jnp.where(zl == 0, kept, taken), jnp.where(zl == 0, taken, kept)], axis=2
    )
    projected = jnp.roll(projected, y, axis=1).reshape(rows, width)
    mixed = tokens.astype(jnp.float32) + normalize(projected, post_gain)
    return mixed.astype(jnp.bfloat16)


def solution(mesh):
    mesh = Mesh(mesh.devices.reshape(EXTENT), AXES)
    row, col = ("y", "zl"), ("x", "zh", "core")
    in_specs = (P(row + col, None), P(), P(), P(row, col), P(row, col), P(col, row))
    out_specs = P(row + col, None)
    return jax.shard_map(
        on_device, mesh=mesh, in_specs=in_specs, out_specs=out_specs, check_vma=False
    )
```
